512 devices in a mesh: row: 32 (over y, x, core), col: 16 (over z).
Axes of the slice: x: 4, y: 4, z: 16, core: 2. Of those that a mesh axis runs over, the one named last changes fastest.
Arguments:
- vertex: float32 [8192, 8192], P('row', 'col'), may hold values from -0.046875 to 0.046875
- bubbles: float32 [4, 8192, 8192], P(None, 'row', 'col'), may hold values from 0.5 to 1.5
- site_panel: float32 [8192, 256], P('row', 'col'), may hold values from -6 to 6
- bond_sites: int32 [24576, 2], replicated, may hold values from 0 to 8191
- bond_class: int32 [24576], replicated, may hold values from 0 to 15
- coupling: float32 [16], replicated, may hold values from -4 to 4
Outputs:
- first_term: float32 [8192, 256], P('col', 'row')
- second_term: float32 [8192, 256], P('row', 'col')
- third_term: float32 [8192, 256], P('col', 'row')
- fourth_term: float32 [8192, 256], P('row', 'col')
The draws below stay inside these ranges and needn't reach their ends.
All inputs are finite; a program needn't handle non-finite values.
Results may differ from the reference program's by a relative error of at most 0.0001.
Values sent between devices are 32-bit elements; how exact they have to be, the bound alone decides.
No kernel may reach another device: no remote copies, remote signals or barrier semaphores. Data moves between devices by JAX's collectives and lax.ppermute only.
A program may use at most 64 MiB of HBM per device.

```python
import jax
import jax.numpy as jnp
from jax import lax

N = 8192
K = 256
LOOPS = 4
CLASSES = 16
NB = 24576


def place_ends(values, stream_key, smallest, largest):
    dims = values.shape
    index_at = [jax.random.randint(jax.random.fold_in(stream_key, axis), (), 0, dims[axis]) for axis in range(len(dims))]
    values = values.at[tuple(index_at)].set(smallest)
    longest = dims.index(max(dims))
    index_at[longest] = (index_at[longest] + 1) % dims[longest]
    return values.at[tuple(index_at)].set(largest)


def shard_levels(stream_key, dims, shards, least, high):
    level = 1.0
    for dim, parts in shards:
        draws = jax.random.uniform(jax.random.fold_in(jax.random.fold_in(stream_key, 6), dim), (parts,), jnp.float32, least / len(shards), high / len(shards))
        level = level * jnp.repeat(jnp.exp(draws), dims[dim] // parts).reshape((-1,) + (1,) * (len(dims) - 1 - dim))
    return level


def gaussian(rng, dims, deviation, reach, split=(), kind=jnp.bfloat16):
    gain = shard_levels(rng, dims, split, -0.22, 0.18) if split else 1.0
    values = jax.random.normal(rng, dims, jnp.float32) * deviation * gain
    return jnp.minimum(jnp.maximum(values, -reach), reach).astype(kind)


def setup_inputs(seed: int = 0) -> dict:
    key_list = jax.random.split(jax.random.key(seed), 7)
    vertex = gaussian(key_list[0], (N, N), (2 * N) ** -0.5, 0.046875, ((0, 32), (1, 16)), jnp.float32)
    bubbles = jnp.clip(0.5 + 1.0 * jax.random.uniform(key_list[1], (LOOPS, N, N), jnp.float32) ** shard_levels(key_list[1], (LOOPS, N, N), ((1, 32), (2, 16)), -0.2, 0.2), 0.5, 1.5)
    site_panel = gaussian(key_list[2], (N, K), 1.0, 6.0, ((0, 32), (1, 16)), jnp.float32)
    bond_sites = place_ends(jax.random.randint(key_list[3], (NB, 2), 0, N), jax.random.fold_in(key_list[3], 1), 0, N - 1).astype(jnp.int32)
    bond_class = place_ends(jax.random.randint(key_list[4], (NB,), 0, CLASSES), jax.random.fold_in(key_list[4], 1), 0, CLASSES - 1).astype(jnp.int32)
    coupling = gaussian(key_list[5], (CLASSES,), 0.25, 4.0, (), jnp.float32)
    return dict(vertex=vertex, bubbles=bubbles, site_panel=site_panel, bond_sites=bond_sites, bond_class=bond_class, coupling=coupling)


def reference(vertex, bubbles, site_panel, bond_sites, bond_class, coupling):
    highest = lax.Precision.HIGHEST
    strength = coupling[bond_class]
    first_site = bond_sites[:, 0]
    second_site = bond_sites[:, 1]
    full = vertex.at[first_site, second_site].add(strength)
    full = full.at[second_site, first_site].add(strength)
    current = site_panel
    results = []
    for step in range(LOOPS):
        weighted = bubbles[step] * full
        if step % 2 == 0:
            weighted = weighted.T
        current = jnp.dot(weighted, current, precision=highest, preferred_element_type=jnp.float32)
        results.append(current)
    return (results[0], results[1], results[2], results[3])
```

```python
import jax
import jax.numpy as jnp
from jax import lax
from jax.experimental import pallas as pl
from jax.experimental.pallas import tpu as pltpu
from jax.sharding import PartitionSpec as P

HIGHEST = lax.Precision.HIGHEST
LANES = 128
SLOTS = 8


def place_kernel(corner, coupling, sites, classes, vertex, full, rank, key, pull):
    rows, cols = vertex.shape
    groups = classes.shape[0]
    first = sites[pl.ds(0, groups, stride=2), :] if sites.ndim == 2 else sites[0]
    second = sites[pl.ds(1, groups, stride=2), :] if sites.ndim == 2 else sites[1]
    kind = classes[...]
    strength = jnp.zeros(kind.shape, jnp.float32)
    for index in range(coupling.shape[0]):
        strength = jnp.where(kind == index, coupling[index], strength)
    pull[...] = strength
    count = jnp.zeros((8, LANES), jnp.int32)
    for way, (end, start) in enumerate(((first, second), (second, first))):
        row = end - corner[0]
        col = start - corner[1]
        inside = (row >= 0) & (row < rows) & (col >= 0) & (col < cols)
        key[pl.ds(way * groups, groups), :] = row * cols + col
        hit = inside.astype(jnp.int32)
        for step in range(groups // 8):
            now = hit[8 * step : 8 * step + 8]
            rank[pl.ds(way * groups + 8 * step, 8), :] = jnp.where(now == 1, count, -(1 << 20))
            count = count + now
    before = jnp.zeros((1, LANES), jnp.int32)
    offsets = []
    for sub in range(8):
        offsets.append(before)
        before = before + count[sub : sub + 1]
    offset = jnp.concatenate(offsets, axis=0)
    for step in range(2 * groups // 8):
        rank[pl.ds(8 * step, 8), :] = rank[pl.ds(8 * step, 8), :] + offset
    most = jnp.max(before)
    full[...] = vertex[...]

    def add(turn, carry):
        row_at = lax.broadcasted_iota(jnp.int32, (rows, LANES), 0)
        col_at = lax.broadcasted_iota(jnp.int32, (cols, LANES), 0)
        ends, starts = [], [[], [], []]
        for slot in range(SLOTS):
            want = turn * SLOTS + slot
            keys = jnp.zeros((8, LANES), jnp.int32)
            pulls = jnp.zeros((8, LANES), jnp.float32)
            for step in range(2 * groups // 8):
                mine = rank[pl.ds(8 * step, 8), :] == want
                at = 8 * step % groups
                keys = keys + jnp.where(mine, key[pl.ds(8 * step, 8), :] + 1, 0)
                pulls = pulls + jnp.where(mine, pull[pl.ds(at, 8), :], 0.0)
            spot = jnp.sum(keys, axis=0, keepdims=True) - 1
            force = jnp.sum(pulls, axis=0, keepdims=True)
            row = spot >> (cols.bit_length() - 1)
            col = spot & (cols - 1)
            ends.append((row_at == row).astype(jnp.float32).astype(jnp.bfloat16))
            here = col_at == col
            rest = force
            for part in range(3):
                piece = rest.astype(jnp.bfloat16).astype(jnp.float32)
                starts[part].append(jnp.where(here, piece, 0.0).astype(jnp.bfloat16))
                rest = rest - piece
        left = jnp.concatenate(ends, axis=1)
        total = full[...]
        for part in range(3):
            total = total + lax.dot_general(
                left,
                jnp.concatenate(starts[part], axis=1),
                (((1,), (1,)), ((), ())),
                preferred_element_type=jnp.float32,
            )
        full[...] = total
        return carry

    lax.fori_loop(0, (most + SLOTS - 1) // SLOTS, add, 0)


def place(vertex, sites, classes, coupling, corner):
    groups = classes.shape[0]
    whole = pl.BlockSpec(memory_space=pltpu.VMEM)
    scalars = pl.BlockSpec(memory_space=pltpu.SMEM)
    return pl.pallas_call(
        place_kernel,
        out_shape=jax.ShapeDtypeStruct(vertex.shape, jnp.float32),
        in_specs=[scalars, scalars, whole, whole, whole],
        out_specs=whole,
        scratch_shapes=[
            pltpu.VMEM((2 * groups, LANES), jnp.int32),
            pltpu.VMEM((2 * groups, LANES), jnp.int32),
            pltpu.VMEM((groups, LANES), jnp.float32),
        ],
        compiler_params=pltpu.CompilerParams(vmem_limit_bytes=32 * 1024 * 1024),
    )(corner, coupling, sites, classes, vertex)


def gather(piece, axis, parts):
    sent = jnp.broadcast_to(piece[None], (parts, *piece.shape))
    return lax.all_to_all(sent, axis, 0, 0).reshape(parts * piece.shape[0], -1)


def scatter_sum(partial_value, axis, parts):
    pieces = partial_value.reshape(parts, partial_value.shape[0] // parts, -1)
    return jnp.sum(lax.all_to_all(pieces, axis, 0, 0), axis=0)


def make(rows_n, cols_n):
    def per_device(vertex, bubbles, site_panel, bond_sites, bond_class, coupling):
        rows_blk, cols_blk = vertex.shape
        corner = jnp.stack(
            [lax.axis_index("row") * rows_blk, lax.axis_index("col") * cols_blk]
        ).astype(jnp.int32)
        groups = bond_class.shape[0] // LANES
        sites = bond_sites.reshape(groups, LANES, 2).transpose(0, 2, 1).reshape(2 * groups, LANES)
        full = place(vertex, sites, bond_class.reshape(groups, LANES), coupling, corner)
        results = []
        current = site_panel.T
        for couple in range(2):
            known = gather(current, "col", cols_n)
            partial_value = jnp.dot(
                known, bubbles[2 * couple] * full, precision=HIGHEST, preferred_element_type=jnp.float32
            )
            odd_term = scatter_sum(partial_value, "row", rows_n)
            known = gather(odd_term, "row", rows_n)
            partial_value = lax.dot_general(
                known,
                bubbles[2 * couple + 1] * full,
                (((1,), (1,)), ((), ())),
                precision=HIGHEST,
                preferred_element_type=jnp.float32,
            )
            current = scatter_sum(partial_value, "col", cols_n)
            results += [odd_term.T, current.T]
        return tuple(results)

    return per_device


def solution(mesh):
    in_specs = (P("row", "col"), P(None, "row", "col"), P("row", "col"), P(), P(), P())
    out_specs = (P("col", "row"), P("row", "col"), P("col", "row"), P("row", "col"))
    return jax.shard_map(
        make(mesh.shape["row"], mesh.shape["col"]),
        mesh=mesh,
        in_specs=in_specs,
        out_specs=out_specs,
        check_vma=False,
    )
```

```python
import jax
import jax.numpy as jnp
from jax import lax
from jax.experimental import pallas as pl
from jax.experimental.pallas import tpu as pltpu
from jax.sharding import Mesh, PartitionSpec as P

HIGHEST = lax.Precision.HIGHEST
LANES = 128
SLOTS = 8


def place_kernel(
    corner, coupling, sites_far, classes_far, mine_far, other_far, own_far, others_far, *rest
):
    loops = own_far.shape[0]
    weighted_far = rest[:loops]
    sites, classes, full, bubbles, rank, key, pull, arrived, left_off = rest[loops:]
    rows, cols = full.shape
    half = rows // 2
    groups = classes.shape[0]
    copies = [
        pltpu.make_async_copy(far, near, arrived.at[index])
        for index, (far, near) in enumerate(
            (
                (sites_far, sites),
                (classes_far, classes),
                (mine_far, full.at[pl.ds(0, half)]),
                (other_far, full.at[pl.ds(half, half)]),
                (own_far, bubbles.at[:, pl.ds(0, half)]),
                (others_far, bubbles.at[:, pl.ds(half, half)]),
            )
        )
    ]
    for copy in copies:
        copy.start()
    copies[0].wait()
    copies[1].wait()
    first = sites[pl.ds(0, groups, stride=2), :]
    second = sites[pl.ds(1, groups, stride=2), :]
    kind = classes[...]
    strength = jnp.zeros(kind.shape, jnp.float32)
    for index in range(coupling.shape[0]):
        strength = jnp.where(kind == index, coupling[index], strength)
    pull[...] = strength
    count = jnp.zeros((8, LANES), jnp.int32)
    for way, (end, start) in enumerate(((first, second), (second, first))):
        row = end - corner[0]
        col = start - corner[1]
        inside = (row >= 0) & (row < rows) & (col >= 0) & (col < cols)
        key[pl.ds(way * groups, groups), :] = (row ^ corner[2]) * cols + col
        hit = inside.astype(jnp.int32)
        for step in range(groups // 8):
            now = hit[8 * step : 8 * step + 8]
            rank[pl.ds(way * groups + 8 * step, 8), :] = jnp.where(now == 1, count, -(1 << 20))
            count = count + now
    before = jnp.zeros((1, LANES), jnp.int32)
    offsets = []
    for sub in range(8):
        offsets.append(before)
        before = before + count[sub : sub + 1]
    offset = jnp.concatenate(offsets, axis=0)
    for step in range(2 * groups // 8):
        rank[pl.ds(8 * step, 8), :] = rank[pl.ds(8 * step, 8), :] + offset
    most = jnp.max(before)
    copies[2].wait()
    copies[3].wait()

    def add(turn, carry):
        row_at = lax.broadcasted_iota(jnp.int32, (rows, LANES), 0)
        col_at = lax.broadcasted_iota(jnp.int32, (cols, LANES), 0)
        ends, starts = [], [[], [], []]
        for slot in range(SLOTS):
            want = turn * SLOTS + slot
            keys = jnp.zeros((8, LANES), jnp.int32)
            pulls = jnp.zeros((8, LANES), jnp.float32)
            for step in range(2 * groups // 8):
                mine = rank[pl.ds(8 * step, 8), :] == want
                at = 8 * step % groups
                keys = keys + jnp.where(mine, key[pl.ds(8 * step, 8), :] + 1, 0)
                pulls = pulls + jnp.where(mine, pull[pl.ds(at, 8), :], 0.0)
            spot = jnp.sum(keys, axis=0, keepdims=True) - 1
            force = jnp.sum(pulls, axis=0, keepdims=True)
            row = spot >> (cols.bit_length() - 1)
            col = spot & (cols - 1)
            ends.append((row_at == row).astype(jnp.float32).astype(jnp.bfloat16))
            here = col_at == col
            rest = force
            for part in range(3):
                piece = rest.astype(jnp.bfloat16).astype(jnp.float32)
                starts[part].append(jnp.where(here, piece, 0.0).astype(jnp.bfloat16))
                rest = rest - piece
        left = jnp.concatenate(ends, axis=1)
        total = full[...]
        for part in range(3):
            total = total + lax.dot_general(
                left,
                jnp.concatenate(starts[part], axis=1),
                (((1,), (1,)), ((), ())),
                preferred_element_type=jnp.float32,
            )
        full[...] = total
        return carry

    lax.fori_loop(0, (most + SLOTS - 1) // SLOTS, add, 0)
    copies[4].wait()
    copies[5].wait()
    leaving = []
    for step in range(loops):
        bubbles[step] = bubbles[step] * full[...]
        leaving.append(pltpu.make_async_copy(bubbles.at[step], weighted_far[step], left_off.at[step]))
        leaving[-1].start()
    for copy in leaving:
        copy.wait()


def place(vertex, other_vertex, bubbles, other_bubbles, sites, classes, coupling, corner):
    half, cols = vertex.shape
    groups = classes.shape[0]
    far = pl.BlockSpec(memory_space=pl.ANY)
    scalars = pl.BlockSpec(memory_space=pltpu.SMEM)
    loops = bubbles.shape[0]
    return pl.pallas_call(
        place_kernel,
        out_shape=[jax.ShapeDtypeStruct((2 * half, cols), jnp.float32)] * loops,
        in_specs=[scalars, scalars] + [far] * 6,
        out_specs=[far] * loops,
        scratch_shapes=[
            pltpu.VMEM(sites.shape, jnp.int32),
            pltpu.VMEM(classes.shape, jnp.int32),
            pltpu.VMEM((2 * half, cols), jnp.float32),
            pltpu.VMEM((loops, 2 * half, cols), jnp.float32),
            pltpu.VMEM((2 * groups, LANES), jnp.int32),
            pltpu.VMEM((2 * groups, LANES), jnp.int32),
            pltpu.VMEM((groups, LANES), jnp.float32),
            pltpu.SemaphoreType.DMA((6,)),
            pltpu.SemaphoreType.DMA((loops,)),
        ],
        compiler_params=pltpu.CompilerParams(vmem_limit_bytes=59 * 1024 * 1024),
    )(corner, coupling, sites, classes, vertex, other_vertex, bubbles, other_bubbles)


def gather(piece, axis, parts):
    sent = jnp.broadcast_to(piece[None], (parts, *piece.shape))
    return lax.all_to_all(sent, axis, 0, 0).reshape(parts * piece.shape[0], -1)


def scatter_sum(partial_value, axis, parts):
    pieces = partial_value.reshape(parts, partial_value.shape[0] // parts, -1)
    return jnp.sum(lax.all_to_all(pieces, axis, 0, 0), axis=0)


def make(chips, cols_n):
    swap = [(0, 1), (1, 0)]

    def per_device(vertex, bubbles, site_panel, bond_sites, bond_class, coupling):
        half, cols_blk = vertex.shape
        core = lax.axis_index("core")
        corner = jnp.stack(
            [lax.axis_index("chip") * 2 * half, lax.axis_index("col") * cols_blk, core * half]
        ).astype(jnp.int32)
        groups = bond_class.shape[0] // LANES
        sites = bond_sites.reshape(groups, LANES, 2).transpose(0, 2, 1).reshape(2 * groups, LANES)
        panels = lax.all_gather(site_panel.T, "core")
        wide = panels.reshape(2, 2, panels.shape[1] // 2, half)
        held = jnp.where(core == 0, wide[:, 0], wide[:, 1])
        current = jnp.where(
            core == 0,
            jnp.concatenate([held[0], held[1]], axis=1),
            jnp.concatenate([held[1], held[0]], axis=1),
        )
        sent = jnp.broadcast_to(current[None], (cols_n, *current.shape))
        sent, sent_vertex, sent_bubbles = lax.optimization_barrier((sent, vertex, bubbles))
        known = lax.all_to_all(sent, "col", 0, 0).reshape(-1, 2 * half)
        weighted = place(
            vertex,
            lax.ppermute(sent_vertex, "core", swap),
            bubbles,
            lax.ppermute(sent_bubbles, "core", swap),
            sites,
            bond_class.reshape(groups, LANES),
            coupling,
            corner,
        )
        odd_terms, even_terms = [], []
        for couple in range(2):
            partial_value = jnp.dot(
                known, weighted[2 * couple], precision=HIGHEST, preferred_element_type=jnp.float32
            )
            odd_term = scatter_sum(partial_value, "chip", chips)
            odd_terms.append(odd_term.T)
            partial_value = lax.dot_general(
                gather(odd_term, "chip", chips),
                weighted[2 * couple + 1],
                (((1,), (1,)), ((), ())),
                precision=HIGHEST,
                preferred_element_type=jnp.float32,
            )
            current = scatter_sum(partial_value, "col", cols_n)
            even_terms.append(current)
            if couple == 0:
                known = gather(current, "col", cols_n)
        both = lax.all_gather(jnp.stack(even_terms), "core")
        swapped = jnp.where(core == 0, both[0, :, :, :half], both[0, :, :, half:])
        straight = jnp.where(core == 0, both[1, :, :, half:], both[1, :, :, :half])
        even_terms = jnp.concatenate([swapped, straight], axis=1)
        return odd_terms[0], even_terms[0].T, odd_terms[1], even_terms[1].T

    return per_device


def solution(mesh):
    chips, cols_n = mesh.shape["row"] // 2, mesh.shape["col"]
    inner = Mesh(mesh.devices.reshape(chips, 2, cols_n), ("chip", "core", "col"))
    row = ("chip", "core")
    in_specs = (P(row, "col"), P(None, row, "col"), P(row, "col"), P(), P(), P())
    out_specs = (P("col", row), P(row, "col"), P("col", row), P(row, "col"))
    return jax.shard_map(
        make(chips, cols_n), mesh=inner, in_specs=in_specs, out_specs=out_specs, check_vma=False
    )
```

```python
import jax
import jax.numpy as jnp
from jax import lax
from jax.experimental import pallas as pl
from jax.experimental.pallas import tpu as pltpu
from jax.sharding import Mesh, PartitionSpec as P

HIGHEST = lax.Precision.HIGHEST
LANES = 128
SLOTS = 8


def fetch(pairs, arrived):
    copies = [
        pltpu.make_async_copy(far, near, arrived.at[index]) for index, (far, near) in enumerate(pairs)
    ]
    for copy in copies:
        copy.start()
    return copies


def place_kernel(
    corner, coupling, sites_far, classes_far, vertex_far, full, sites, classes, rank, key, pull, arrived
):
    rows, cols = full.shape
    groups = classes.shape[0]
    copies = fetch(((sites_far, sites), (classes_far, classes), (vertex_far, full)), arrived)
    copies[0].wait()
    copies[1].wait()
    first = sites[pl.ds(0, groups, stride=2), :]
    second = sites[pl.ds(1, groups, stride=2), :]
    kind = classes[...]
    strength = jnp.zeros(kind.shape, jnp.float32)
    for index in range(coupling.shape[0]):
        strength = jnp.where(kind == index, coupling[index], strength)
    pull[...] = strength
    count = jnp.zeros((8, LANES), jnp.int32)
    for way, (end, start) in enumerate(((first, second), (second, first))):
        row = end - corner[0]
        col = start - corner[1]
        inside = (row >= 0) & (row < rows) & (col >= 0) & (col < cols)
        key[pl.ds(way * groups, groups), :] = row * cols + col
        hit = inside.astype(jnp.int32)
        for step in range(groups // 8):
            now = hit[8 * step : 8 * step + 8]
            rank[pl.ds(way * groups + 8 * step, 8), :] = jnp.where(now == 1, count, -(1 << 20))
            count = count + now
    before = jnp.zeros((1, LANES), jnp.int32)
    offsets = []
    for sub in range(8):
        offsets.append(before)
        before = before + count[sub : sub + 1]
    offset = jnp.concatenate(offsets, axis=0)
    for step in range(2 * groups // 8):
        rank[pl.ds(8 * step, 8), :] = rank[pl.ds(8 * step, 8), :] + offset
    most = jnp.max(before)
    copies[2].wait()

    def add(turn, carry):
        row_at = lax.broadcasted_iota(jnp.int32, (rows, LANES), 0)
        col_at = lax.broadcasted_iota(jnp.int32, (cols, LANES), 0)
        ends, starts = [], [[], [], []]
        for slot in range(SLOTS):
            want = turn * SLOTS + slot
            keys = jnp.zeros((8, LANES), jnp.int32)
            pulls = jnp.zeros((8, LANES), jnp.float32)
            for step in range(2 * groups // 8):
                mine = rank[pl.ds(8 * step, 8), :] == want
                at = 8 * step % groups
                keys = keys + jnp.where(mine, key[pl.ds(8 * step, 8), :] + 1, 0)
                pulls = pulls + jnp.where(mine, pull[pl.ds(at, 8), :], 0.0)
            spot = jnp.sum(keys, axis=0, keepdims=True) - 1
            force = jnp.sum(pulls, axis=0, keepdims=True)
            row = spot >> (cols.bit_length() - 1)
            col = spot & (cols - 1)
            ends.append((row_at == row).astype(jnp.float32).astype(jnp.bfloat16))
            here = col_at == col
            rest = force
            for part in range(3):
                piece = rest.astype(jnp.bfloat16).astype(jnp.float32)
                starts[part].append(jnp.where(here, piece, 0.0).astype(jnp.bfloat16))
                rest = rest - piece
        left = jnp.concatenate(ends, axis=1)
        total = full[...]
        for part in range(3):
            total = total + lax.dot_general(
                left,
                jnp.concatenate(starts[part], axis=1),
                (((1,), (1,)), ((), ())),
                preferred_element_type=jnp.float32,
            )
        full[...] = total
        return carry

    lax.fori_loop(0, (most + SLOTS - 1) // SLOTS, add, 0)


def place(vertex, sites, classes, coupling, corner):
    groups = classes.shape[0]
    far = pl.BlockSpec(memory_space=pl.ANY)
    scalars = pl.BlockSpec(memory_space=pltpu.SMEM)
    sites, classes, vertex = (
        pltpu.with_memory_space_constraint(array, pltpu.HBM) for array in (sites, classes, vertex)
    )
    return pl.pallas_call(
        place_kernel,
        out_shape=pltpu.VMEM(vertex.shape, jnp.float32),
        in_specs=[scalars, scalars] + [far] * 3,
        out_specs=pl.BlockSpec(memory_space=pltpu.VMEM),
        scratch_shapes=[
            pltpu.VMEM(sites.shape, jnp.int32),
            pltpu.VMEM(classes.shape, jnp.int32),
            pltpu.VMEM((2 * groups, LANES), jnp.int32),
            pltpu.VMEM((2 * groups, LANES), jnp.int32),
            pltpu.VMEM((groups, LANES), jnp.float32),
            pltpu.SemaphoreType.DMA((3,)),
        ],
        cost_estimate=pl.CostEstimate(flops=20 * 10**9, bytes_accessed=10**6, transcendentals=0),
        compiler_params=pltpu.CompilerParams(vmem_limit_bytes=24 * 1024 * 1024),
    )(corner, coupling, sites, classes, vertex)


def weigh_kernel(own_full, other_full, own_far, others_far, *rest):
    loops, half = own_far.shape[:2]
    weighted_far, (weighted, bubbles, gone, arrived) = rest[:loops], rest[loops:]
    copies = fetch(
        [
            (far.at[step], bubbles.at[step, pl.ds(half * index, half)])
            for step in range(loops)
            for index, far in enumerate((own_far, others_far))
        ],
        arrived,
    )
    leaving = []
    for step in range(loops):
        for index, full in enumerate((own_full, other_full)):
            copies[2 * step + index].wait()
            rows = pl.ds(half * index, half)
            product = bubbles[step, rows, :] * full[...]
            if step % 2:
                weighted[step, :, rows] = product.T
            else:
                weighted[step, rows, :] = product
        leaving.append(pltpu.make_async_copy(weighted.at[step], weighted_far[step], gone.at[step]))
        leaving[-1].start()
    for copy in leaving:
        copy.wait()


def weigh(own_full, other_full, bubbles, other_bubbles):
    loops, half, cols = bubbles.shape
    near = pl.BlockSpec(memory_space=pltpu.VMEM)
    far = pl.BlockSpec(memory_space=pl.ANY)
    return pl.pallas_call(
        weigh_kernel,
        out_shape=[jax.ShapeDtypeStruct((2 * half, cols), jnp.float32)] * loops,
        in_specs=[near, near, far, far],
        out_specs=[far] * loops,
        scratch_shapes=[
            pltpu.VMEM((loops, 2 * half, cols), jnp.float32),
            pltpu.VMEM((loops, 2 * half, cols), jnp.float32),
            pltpu.SemaphoreType.DMA((loops,)),
            pltpu.SemaphoreType.DMA((2 * loops,)),
        ],
        cost_estimate=pl.CostEstimate(
            flops=2 * loops * half * cols, bytes_accessed=16 * loops * half * cols, transcendentals=0
        ),
        compiler_params=pltpu.CompilerParams(vmem_limit_bytes=24 * 1024 * 1024),
    )(own_full, other_full, pltpu.with_memory_space_constraint(bubbles, pltpu.HBM), other_bubbles)


def product_kernel(known, weighted, out):
    product = jnp.dot(
        known[...].reshape(-1, known.shape[2]),
        weighted[...],
        precision=HIGHEST,
        preferred_element_type=jnp.float32,
    )
    out[...] = product.reshape(out.shape)


def product(known, weighted):
    near = pl.BlockSpec(memory_space=pltpu.VMEM)
    return pl.pallas_call(
        product_kernel,
        out_shape=jax.ShapeDtypeStruct(known.shape, jnp.float32),
        in_specs=[near, near],
        out_specs=near,
        compiler_params=pltpu.CompilerParams(vmem_limit_bytes=16 * 1024 * 1024),
    )(known, weighted)


def gather(piece, axis, parts):
    return lax.all_to_all(jnp.broadcast_to(piece[None], (parts, *piece.shape)), axis, 0, 0)


def scatter_sum(pieces, axis):
    return jnp.sum(lax.all_to_all(pieces, axis, 0, 0), axis=0)


def make(chips, cols_n):
    swap = [(0, 1), (1, 0)]

    def per_device(vertex, bubbles, site_panel, bond_sites, bond_class, coupling):
        half, cols_blk = vertex.shape
        core = lax.axis_index("core")
        corner = jnp.stack(
            [lax.axis_index(("chip", "core")) * half, lax.axis_index("col") * cols_blk]
        ).astype(jnp.int32)
        groups = bond_class.shape[0] // LANES
        sites = bond_sites.reshape(groups, LANES, 2).transpose(0, 2, 1).reshape(2 * groups, LANES)
        panels = lax.all_gather(site_panel.T, "core")
        wide = panels.reshape(2, 2, panels.shape[1] // 2, half)
        held = jnp.where(core == 0, wide[:, 0], wide[:, 1])
        current = jnp.where(
            core == 0,
            jnp.concatenate([held[0], held[1]], axis=1),
            jnp.concatenate([held[1], held[0]], axis=1),
        )
        sent = jnp.broadcast_to(current[None], (cols_n, *current.shape))
        sent, corner, sent_bubbles = lax.optimization_barrier((sent, corner, bubbles))
        known = lax.all_to_all(sent, "col", 0, 0)
        full = place(vertex, sites, bond_class.reshape(groups, LANES), coupling, corner)
        weighted = weigh(
            full,
            lax.ppermute(full, "core", swap),
            bubbles,
            lax.ppermute(sent_bubbles, "core", swap),
        )
        first = scatter_sum(product(known, weighted[0]), "chip")
        second = scatter_sum(product(gather(first, "chip", chips), weighted[1]), "col")
        third = scatter_sum(product(gather(second, "col", cols_n), weighted[2]), "chip")
        fourth = scatter_sum(product(gather(third, "chip", chips), weighted[3]), "col")
        both = lax.all_gather(jnp.stack([second, fourth]), "core")
        swapped = jnp.where(core == 0, both[0, :, :, :half], both[0, :, :, half:])
        straight = jnp.where(core == 0, both[1, :, :, half:], both[1, :, :, :half])
        even_terms = jnp.concatenate([swapped, straight], axis=1)
        return first.T, even_terms[0].T, third.T, even_terms[1].T

    return per_device


def solution(mesh):
    chips, cols_n = mesh.shape["row"] // 2, mesh.shape["col"]
    inner = Mesh(mesh.devices.reshape(chips, 2, cols_n), ("chip", "core", "col"))
    row = ("chip", "core")
    in_specs = (P(row, "col"), P(None, row, "col"), P(row, "col"), P(), P(), P())
    out_specs = (P("col", row), P(row, "col"), P("col", row), P(row, "col"))
    return jax.shard_map(
        make(chips, cols_n), mesh=inner, in_specs=in_specs, out_specs=out_specs, check_vma=False
    )
```

```python
import functools

import jax
import jax.numpy as jnp
from jax import lax
from jax.experimental import pallas as pl
from jax.experimental.pallas import tpu as pltpu
from jax.sharding import Mesh, PartitionSpec as P

HIGHEST = lax.Precision.HIGHEST
LANES = 128
SLOTS = 8


def fetch(pairs, arrived):
    copies = [
        pltpu.make_async_copy(far, near, arrived.at[index]) for index, (far, near) in enumerate(pairs)
    ]
    for copy in copies:
        copy.start()
    return copies


def place_kernel(
    corner, coupling, sites_far, classes_far, vertex_far, full, sites, classes, rank, key, pull, arrived
):
    rows, cols = full.shape
    groups = classes.shape[0]
    copies = fetch(((sites_far, sites), (classes_far, classes), (vertex_far, full)), arrived)
    copies[0].wait()
    copies[1].wait()
    first = sites[pl.ds(0, groups, stride=2), :]
    second = sites[pl.ds(1, groups, stride=2), :]
    kind = classes[...]
    strength = jnp.zeros(kind.shape, jnp.float32)
    for index in range(coupling.shape[0]):
        strength = jnp.where(kind == index, coupling[index], strength)
    pull[...] = strength
    count = jnp.zeros((8, LANES), jnp.int32)
    for way, (end, start) in enumerate(((first, second), (second, first))):
        row = end - corner[0]
        col = start - corner[1]
        inside = (row >= 0) & (row < rows) & (col >= 0) & (col < cols)
        key[pl.ds(way * groups, groups), :] = row * cols + col
        hit = inside.astype(jnp.int32)
        for step in range(groups // 8):
            now = hit[8 * step : 8 * step + 8]
            rank[pl.ds(way * groups + 8 * step, 8), :] = jnp.where(now == 1, count, -(1 << 20))
            count = count + now
    before = jnp.zeros((1, LANES), jnp.int32)
    offsets = []
    for sub in range(8):
        offsets.append(before)
        before = before + count[sub : sub + 1]
    offset = jnp.concatenate(offsets, axis=0)
    for step in range(2 * groups // 8):
        rank[pl.ds(8 * step, 8), :] = rank[pl.ds(8 * step, 8), :] + offset
    most = jnp.max(before)
    copies[2].wait()

    def add(turn, carry):
        row_at = lax.broadcasted_iota(jnp.int32, (rows, LANES), 0)
        col_at = lax.broadcasted_iota(jnp.int32, (cols, LANES), 0)
        ends, starts = [], [[], [], []]
        for slot in range(SLOTS):
            want = turn * SLOTS + slot
            keys = jnp.zeros((8, LANES), jnp.int32)
            pulls = jnp.zeros((8, LANES), jnp.float32)
            for step in range(2 * groups // 8):
                mine = rank[pl.ds(8 * step, 8), :] == want
                at = 8 * step % groups
                keys = keys + jnp.where(mine, key[pl.ds(8 * step, 8), :] + 1, 0)
                pulls = pulls + jnp.where(mine, pull[pl.ds(at, 8), :], 0.0)
            spot = jnp.sum(keys, axis=0, keepdims=True) - 1
            force = jnp.sum(pulls, axis=0, keepdims=True)
            row = spot >> (cols.bit_length() - 1)
            col = spot & (cols - 1)
            ends.append((row_at == row).astype(jnp.float32).astype(jnp.bfloat16))
            here = col_at == col
            rest = force
            for part in range(3):
                piece = rest.astype(jnp.bfloat16).astype(jnp.float32)
                starts[part].append(jnp.where(here, piece, 0.0).astype(jnp.bfloat16))
                rest = rest - piece
        left = jnp.concatenate(ends, axis=1)
        total = full[...]
        for part in range(3):
            total = total + lax.dot_general(
                left,
                jnp.concatenate(starts[part], axis=1),
                (((1,), (1,)), ((), ())),
                preferred_element_type=jnp.float32,
            )
        full[...] = total
        return carry

    lax.fori_loop(0, (most + SLOTS - 1) // SLOTS, add, 0)


def place(vertex, sites, classes, coupling, corner):
    groups = classes.shape[0]
    far = pl.BlockSpec(memory_space=pl.ANY)
    scalars = pl.BlockSpec(memory_space=pltpu.SMEM)
    sites, classes, vertex = (
        pltpu.with_memory_space_constraint(array, pltpu.HBM) for array in (sites, classes, vertex)
    )
    return pl.pallas_call(
        place_kernel,
        out_shape=pltpu.VMEM(vertex.shape, jnp.float32),
        in_specs=[scalars, scalars] + [far] * 3,
        out_specs=pl.BlockSpec(memory_space=pltpu.VMEM),
        scratch_shapes=[
            pltpu.VMEM(sites.shape, jnp.int32),
            pltpu.VMEM(classes.shape, jnp.int32),
            pltpu.VMEM((2 * groups, LANES), jnp.int32),
            pltpu.VMEM((2 * groups, LANES), jnp.int32),
            pltpu.VMEM((groups, LANES), jnp.float32),
            pltpu.SemaphoreType.DMA((3,)),
        ],
        cost_estimate=pl.CostEstimate(flops=20 * 10**9, bytes_accessed=10**6, transcendentals=0),
        compiler_params=pltpu.CompilerParams(vmem_limit_bytes=24 * 1024 * 1024),
    )(corner, coupling, sites, classes, vertex)


def weigh_kernel(steps, own_full, other_full, own_far, others_far, *rest):
    half = own_far.shape[1]
    outs, (weighted, bubbles, gone, arrived) = rest[: len(steps)], rest[len(steps) :]
    copies = fetch(
        [
            (far.at[step], bubbles.at[place, pl.ds(half * index, half)])
            for place, step in enumerate(steps)
            for index, far in enumerate((own_far, others_far))
        ],
        arrived,
    )
    leaving = []
    for place, step in enumerate(steps):
        stays = len(steps) == 1
        near = outs[0] if stays else weighted.at[place]
        for index, full in enumerate((own_full, other_full)):
            copies[2 * place + index].wait()
            rows = pl.ds(half * index, half)
            product = bubbles[place, rows, :] * full[...]
            if step % 2:
                near[:, rows] = product.T
            else:
                near[rows, :] = product
        if not stays:
            leaving.append(pltpu.make_async_copy(near, outs[place], gone.at[place]))
            leaving[-1].start()
    for copy in leaving:
        copy.wait()


def weigh(steps, own_full, other_full, bubbles, other_bubbles):
    half, cols = bubbles.shape[1:]
    count = len(steps)
    near = pl.BlockSpec(memory_space=pltpu.VMEM)
    far = pl.BlockSpec(memory_space=pl.ANY)
    return pl.pallas_call(
        functools.partial(weigh_kernel, steps),
        out_shape=[jax.ShapeDtypeStruct((2 * half, cols), jnp.float32)] * count,
        in_specs=[near, near, far, far],
        out_specs=[near if count == 1 else far] * count,
        scratch_shapes=[
            pltpu.VMEM((count, 2 * half, cols), jnp.float32),
            pltpu.VMEM((count, 2 * half, cols), jnp.float32),
            pltpu.SemaphoreType.DMA((count,)),
            pltpu.SemaphoreType.DMA((2 * count,)),
        ],
        cost_estimate=pl.CostEstimate(
            flops=2 * count * half * cols, bytes_accessed=16 * count * half * cols, transcendentals=0
        ),
        compiler_params=pltpu.CompilerParams(vmem_limit_bytes=24 * 1024 * 1024),
    )(own_full, other_full, pltpu.with_memory_space_constraint(bubbles, pltpu.HBM), other_bubbles)


def product_kernel(known, weighted, out):
    product = jnp.dot(
        known[...].reshape(-1, known.shape[2]),
        weighted[...],
        precision=HIGHEST,
        preferred_element_type=jnp.float32,
    )
    out[...] = product.reshape(out.shape)


def product(known, weighted):
    near = pl.BlockSpec(memory_space=pltpu.VMEM)
    return pl.pallas_call(
        product_kernel,
        out_shape=jax.ShapeDtypeStruct(known.shape, jnp.float32),
        in_specs=[near, near],
        out_specs=near,
        compiler_params=pltpu.CompilerParams(vmem_limit_bytes=16 * 1024 * 1024),
    )(known, weighted)


def first_kernel(core, known, weighted, out):
    half = known.shape[2]
    product = jnp.dot(
        known[core[0]],
        weighted[pl.ds(0, half), :],
        precision=HIGHEST,
        preferred_element_type=jnp.float32,
    ) + jnp.dot(
        known[1 - core[0]],
        weighted[pl.ds(half, half), :],
        precision=HIGHEST,
        preferred_element_type=jnp.float32,
    )
    out[...] = product.reshape(out.shape)


def first_product(core, known, weighted):
    near = pl.BlockSpec(memory_space=pltpu.VMEM)
    parts, slab, half = known.shape
    return pl.pallas_call(
        first_kernel,
        out_shape=jax.ShapeDtypeStruct((parts // 2, slab, 2 * half), jnp.float32),
        in_specs=[pl.BlockSpec(memory_space=pltpu.SMEM), near, near],
        out_specs=near,
        compiler_params=pltpu.CompilerParams(vmem_limit_bytes=16 * 1024 * 1024),
    )(core, known.reshape(2, -1, half), weighted)


def settle_kernel(core, both, *terms):
    slab, half = both.shape[2], both.shape[3] // 2
    leads = jnp.broadcast_to(core[0], (slab, half)) == 0
    for step, term in enumerate(terms):
        for index in range(2):
            front, back = both[index, step, :, :half], both[index, step, :, half:]
            chosen = jnp.where(leads, back, front) if index else jnp.where(leads, front, back)
            term[pl.ds(slab * index, slab), :] = chosen


def settle(core, both):
    cores, count, slab, rows = both.shape
    near = pl.BlockSpec(memory_space=pltpu.VMEM)
    return pl.pallas_call(
        settle_kernel,
        out_shape=[jax.ShapeDtypeStruct((cores * slab, rows // 2), jnp.float32)] * count,
        in_specs=[pl.BlockSpec(memory_space=pltpu.SMEM), near],
        out_specs=[near] * count,
    )(core, both)


def gather(piece, axis, parts):
    return lax.all_to_all(jnp.broadcast_to(piece[None], (parts, *piece.shape)), axis, 0, 0)


def scatter_sum(pieces, axis):
    return jnp.sum(lax.all_to_all(pieces, axis, 0, 0), axis=0)


def make(chips, cols_n):
    swap = [(0, 1), (1, 0)]

    def per_device(vertex, bubbles, site_panel, bond_sites, bond_class, coupling):
        half, cols_blk = vertex.shape
        core = lax.axis_index("core").astype(jnp.int32).reshape(1)
        corner = jnp.stack(
            [lax.axis_index(("chip", "core")) * half, lax.axis_index("col") * cols_blk]
        ).astype(jnp.int32)
        groups = bond_class.shape[0] // LANES
        sites = bond_sites.reshape(groups, LANES, 2).transpose(0, 2, 1).reshape(2 * groups, LANES)
        slab = site_panel.shape[1] // 2
        sent = jnp.broadcast_to(
            site_panel.T.reshape(2, 1, slab, half), (2, cols_n, slab, half)
        ).reshape(2 * cols_n, slab, half)
        sent, corner, sent_bubbles = lax.optimization_barrier((sent, corner, bubbles))
        known = lax.all_to_all(sent, ("core", "col"), 0, 0)
        full = place(vertex, sites, bond_class.reshape(groups, LANES), coupling, corner)
        blocks = (
            full,
            lax.ppermute(full, "core", swap),
            bubbles,
            lax.ppermute(sent_bubbles, "core", swap),
        )
        later = weigh(tuple(range(1, bubbles.shape[0])), *blocks)
        own_full, later = lax.optimization_barrier((blocks[0], later))
        weighted = weigh((0,), own_full, *blocks[1:]) + tuple(later)
        first = scatter_sum(first_product(core, known, weighted[0]), "chip")
        second = scatter_sum(product(gather(first, "chip", chips), weighted[1]), "col")
        third = scatter_sum(product(gather(second, "col", cols_n), weighted[2]), "chip")
        fourth = scatter_sum(product(gather(third, "chip", chips), weighted[3]), "col")
        both = lax.all_gather(jnp.stack([second, fourth]), "core")
        second, fourth = settle(core, both)
        return first.T, second.T, third.T, fourth.T

    return per_device


def solution(mesh):
    chips, cols_n = mesh.shape["row"] // 2, mesh.shape["col"]
    inner = Mesh(mesh.devices.reshape(chips, 2, cols_n), ("chip", "core", "col"))
    row = ("chip", "core")
    in_specs = (P(row, "col"), P(None, row, "col"), P(row, "col"), P(), P(), P())
    out_specs = (P("col", row), P(row, "col"), P("col", row), P(row, "col"))
    return jax.shard_map(
        make(chips, cols_n), mesh=inner, in_specs=in_specs, out_specs=out_specs, check_vma=False
    )
```
